256 devices in a mesh: rows: 4 (over x), hid: 8 (over y, z_lo), wid: 8 (over z_hi, core).
Axes of the slice: x: 4, y: 4, z: 8 (z_hi: 4, z_lo: 2; z = z_hi * 2 + z_lo), core: 2. Of those that a mesh axis runs over, the one named last changes fastest.
Arguments:
- tokens: bfloat16 [1536, 8192], P(('rows', 'hid'), 'wid'), may hold values from -6 to 6
- grad_out: bfloat16 [1536, 8192], P(('rows', 'hid'), 'wid'), may hold values from -0.609375 to 0.609375
- gate_weight: bfloat16 [8192, 16384], P('wid', ('rows', 'hid')), may hold values from -0.0625 to 0.0625
- up_weight: bfloat16 [8192, 16384], P('wid', ('rows', 'hid')), may hold values from -0.0625 to 0.0625
- down_weight: bfloat16 [16384, 8192], P(('rows', 'hid'), 'wid'), may hold values from -0.046875 to 0.046875
Outputs:
- grad_tokens: bfloat16 [1536, 8192], P(('rows', 'hid'), 'wid')
- grad_gate: bfloat16 [8192, 16384], P('wid', ('rows', 'hid'))
- grad_up: bfloat16 [8192, 16384], P('wid', ('rows', 'hid'))
- grad_down: bfloat16 [16384, 8192], P(('rows', 'hid'), 'wid')
The draws below stay inside these ranges and needn't reach their ends.
All inputs are finite; a program needn't handle non-finite values.
Results may differ from the reference program's by a relative error of at most 0.034.
Values may be sent and summed in bfloat16 or wider, within the bound.
No kernel may reach another device: no remote copies, remote signals or barrier semaphores. Data moves between devices by JAX's collectives and lax.ppermute only.
A program may use at most 128 MiB of HBM per device.

```python
import jax
import jax.numpy as jnp
from jax import lax

D = 8192
FF = 16384
ROWS = 384
TOKENS = 1536
N_ROWS = 4
N_WID = 8


def level_of(rng, extent, cuts, low, top_value):
    loudness, own = 1.0, jax.random.fold_in(rng, 6)
    for position, shards_of in cuts:
        draws = jnp.exp(jax.random.uniform(jax.random.fold_in(own, position), (shards_of,), jnp.float32, low / len(cuts), top_value / len(cuts)))
        loudness = loudness * jnp.repeat(draws, extent[position] // shards_of).reshape([-1 if axis == position else 1 for axis in range(len(extent))])
    return loudness


def bell_draw(rng, shape, scale, reach, pieces=(), held_as=jnp.bfloat16):
    loudness = level_of(rng, shape, pieces, -0.22, 0.18) if pieces else 1.0
    drawn = jax.random.normal(rng, shape, jnp.float32) * scale * loudness
    return jnp.minimum(jnp.maximum(drawn, -reach), reach).astype(held_as)


def setup_inputs(seed: int = 0) -> dict:
    keys = jax.random.split(jax.random.key(seed), 6)
    tokens = bell_draw(keys[0], (TOKENS, D), 1.0, 6.0, ((0, 32), (1, 8)))
    grad_out = bell_draw(keys[1], (TOKENS, D), (4.0 / TOKENS ** 0.5), 0.609375, ((0, 32), (1, 8)))
    gate_weight = bell_draw(keys[2], (D, FF), D ** -0.5, 0.0625, ((0, 8), (1, 32)))
    up_weight = bell_draw(keys[3], (D, FF), D ** -0.5, 0.0625, ((0, 8), (1, 32)))
    down_weight = bell_draw(keys[4], (FF, D), FF ** -0.5, 0.046875, ((0, 32), (1, 8)))
    return dict(tokens=tokens, grad_out=grad_out, gate_weight=gate_weight, up_weight=up_weight, down_weight=down_weight)


def width_partials(left, right):
    block = left.shape[1] // N_WID
    total = jnp.zeros((left.shape[0], right.shape[1]), jnp.float32)
    for index in range(N_WID):
        piece = jnp.dot(left[:, index * block:(index + 1) * block], right[index * block:(index + 1) * block, :], preferred_element_type=jnp.float32)
        total = total + lax.optimization_barrier(piece.astype(jnp.bfloat16)).astype(jnp.float32)
    return total


def token_partials(left, right):
    total = jnp.zeros((left.shape[1], right.shape[1]), jnp.float32)
    for index in range(N_ROWS):
        piece = jnp.dot(left[index * ROWS:(index + 1) * ROWS, :].T, right[index * ROWS:(index + 1) * ROWS, :], preferred_element_type=jnp.float32)
        total = total + lax.optimization_barrier(piece.astype(jnp.bfloat16)).astype(jnp.float32)
    return total.astype(jnp.bfloat16)


def reference(tokens, grad_out, gate_weight, up_weight, down_weight):
    gate = width_partials(tokens, gate_weight)
    up = width_partials(tokens, up_weight)
    hidden_grad = width_partials(grad_out, down_weight.T)
    logistic = jax.nn.sigmoid(gate)
    activated = gate * logistic
    hidden = (activated * up).astype(jnp.bfloat16)
    up_grad = (hidden_grad * activated).astype(jnp.bfloat16)
    gate_grad = (hidden_grad * up * logistic * (1.0 + gate * (1.0 - logistic))).astype(jnp.bfloat16)
    grad_tokens = jnp.dot(gate_grad, gate_weight.T, preferred_element_type=jnp.float32) + jnp.dot(up_grad, up_weight.T, preferred_element_type=jnp.float32)
    grad_gate = token_partials(tokens, gate_grad)
    grad_up = token_partials(tokens, up_grad)
    grad_down = token_partials(hidden, grad_out)
    return grad_tokens.astype(jnp.bfloat16), grad_gate, grad_up, grad_down
```

```python
import jax
import jax.numpy as jnp
from jax import lax
from jax.experimental import pallas as pl
from jax.experimental.pallas import tpu as pltpu
from jax.sharding import PartitionSpec as P

BF = jnp.bfloat16
F32 = jnp.float32
IN_VMEM = pl.BlockSpec(memory_space=pltpu.VMEM)
IN_SMEM = pl.BlockSpec(memory_space=pltpu.SMEM)


def swiglu_grads(gate, up, hidden_grad):
    logistic = jax.nn.sigmoid(gate)
    activated = gate * logistic
    hidden = (activated * up).astype(BF)
    up_grad = (hidden_grad * activated).astype(BF)
    gate_grad = (hidden_grad * up * logistic * (1.0 + gate * (1.0 - logistic))).astype(BF)
    return hidden, up_grad, gate_grad


SHARE = 8


def cost(flops, moved, transcendentals=0):
    return pl.CostEstimate(flops=flops // SHARE, bytes_accessed=moved // SHARE, transcendentals=transcendentals)


def dot(left, right, cl, cr):
    return lax.dot_general(left, right, (((cl,), (cr,)), ((), ())), preferred_element_type=F32)


def forward_kernel(first, z_ref, *refs):
    *pieces, wg, wg2, wu, wu2, wd, wd2, keep, later, send, xd, res = refs
    part = pieces[0].shape[0]
    rows = part * len(pieces)
    width, ff = wg.shape
    block = ff // 4
    step = 256
    for index, piece in enumerate(pieces):
        xd[index * part:(index + 1) * part, :] = piece[...]

    def units(n, carry):
        at = pl.ds(pl.multiple_of(n * step, step), step)
        res[0, :, at] = dot(xd[:, :width], wg[:, at], 1, 0) + dot(xd[:, width:2 * width], wg2[:, at], 1, 0)
        res[1, :, at] = dot(xd[:, :width], wu[:, at], 1, 0) + dot(xd[:, width:2 * width], wu2[:, at], 1, 0)
        res[2, :, at] = dot(xd[:, 2 * width:3 * width], wd[at, :], 1, 1) + dot(xd[:, 3 * width:], wd2[at, :], 1, 1)
        return carry

    lax.fori_loop(0, ff // step, units, 0)
    for k, out, row in ((0, keep, 0), (4 - first, later, 0), (first, send, 0), (2, send, rows)):
        at = pl.ds(pl.multiple_of((z_ref[0] ^ k) * block, block), block)
        for index in range(3):
            out[row:row + rows, index * block:(index + 1) * block] = res[index, :, at].astype(out.dtype)


def forward(first, z, pieces, weights):
    part, lanes = pieces[0].shape
    width, ff = weights[0].shape
    rows, cols = part * len(pieces), 3 * ff // 4
    return pl.pallas_call(
        lambda *refs: forward_kernel(first, *refs),
        in_specs=[IN_SMEM] + [IN_VMEM] * (len(pieces) + 6),
        out_specs=[IN_VMEM] * 3,
        scratch_shapes=[pltpu.VMEM((rows, lanes), BF), pltpu.VMEM((3, rows, ff), F32)],
        out_shape=[jax.ShapeDtypeStruct((rows, cols), F32)] * 2 + [jax.ShapeDtypeStruct((2 * rows, cols), BF)],
        compiler_params=pltpu.CompilerParams(vmem_limit_bytes=8 * 2**20),
        cost_estimate=cost(12 * rows * width * ff, 2 * (6 * ff * width + rows * lanes)),
    )(z, *pieces, *weights)


def swiglu_kernel(keep, got, last, out):
    rows, cols = last.shape
    block = cols // 3
    total = keep[...] + got[:rows, :].astype(F32) + last[...].astype(F32)
    parts = swiglu_grads(total[:, :block], total[:, block:2 * block], total[:, 2 * block:])
    for index, part in enumerate(parts):
        out[:, index * block:(index + 1) * block] = part


def swiglu(keep, got, last):
    rows, cols = last.shape
    return pl.pallas_call(
        swiglu_kernel,
        out_shape=jax.ShapeDtypeStruct((rows, cols), BF),
        compiler_params=pltpu.CompilerParams(vmem_limit_bytes=8 * 2**20),
        cost_estimate=cost(20 * rows * cols, 12 * rows * cols, rows * cols),
    )(keep, got, last)


def groups_of(firsts, z_ref, refs):
    top = 0
    for first, pair, rest in zip(firsts, refs[::2], refs[1::2]):
        rows = pair.shape[0] // 2
        block = pair.shape[1] // 3
        for k, ref, row in ((0, pair, 0), (first, pair, rows), (4 - first, rest, 0), (2, rest, rows)):
            at = pl.multiple_of((z_ref[0] ^ k) * block, block)
            yield at, slice(top, top + rows), lambda index, ref=ref, row=row, rows=rows, block=block: ref[
                row:row + rows, index * block:(index + 1) * block
            ]
        top += rows


def input_grad_kernel(firsts, z_ref, *refs):
    count = 2 * len(firsts)
    segments, (wg, wg2, wu, wu2, out_a, out_b, acts) = refs[:count], refs[count:]
    rows = acts.shape[0]
    block = segments[0].shape[1] // 3
    width, ff = wg.shape
    step = 256
    for at, here, value in groups_of(firsts, z_ref, segments):
        acts[here, pl.ds(ff + at, block)] = value(1)
        acts[here, pl.ds(at, block)] = value(2)

    for index, (gate, up) in enumerate(((wg, wu), (wg2, wu2))):
        def columns(n, carry):
            at = pl.multiple_of(n * step, step)
            res = dot(acts[:, :ff], gate[pl.ds(at, step), :], 1, 1)
            res = (res + dot(acts[:, ff:], up[pl.ds(at, step), :], 1, 1)).astype(BF)
            out_a[:, pl.ds(index * width + at, step)] = res[:rows // 2]
            out_b[:, pl.ds(index * width + at, step)] = res[rows // 2:]
            return carry

        lax.fori_loop(0, width // step, columns, 0)


def firsts_and_arrays(segments):
    return [first for first, *_ in segments], [array for _, *arrays in segments for array in arrays]


def input_grad(z, segments, weights):
    firsts, arrays = firsts_and_arrays(segments)
    rows = sum(array.shape[0] for array in arrays) // 4
    width, ff = weights[0].shape
    return pl.pallas_call(
        lambda *refs: input_grad_kernel(firsts, *refs),
        in_specs=[IN_SMEM] + [IN_VMEM] * (len(arrays) + 4),
        out_specs=[IN_VMEM] * 2,
        scratch_shapes=[pltpu.VMEM((rows, 2 * ff), BF)],
        out_shape=[jax.ShapeDtypeStruct((rows // 2, 2 * width), BF)] * 2,
        compiler_params=pltpu.CompilerParams(vmem_limit_bytes=8 * 2**20),
        cost_estimate=cost(8 * rows * width * ff, 4 * (2 * ff * width + rows * width)),
    )(z, *arrays, *weights[:4])


def weight_grad_kernel(firsts, count, partial, z_ref, *refs):
    pieces, refs = refs[:count], refs[count:]
    segments, refs = refs[:2 * len(firsts)], refs[2 * len(firsts):]
    before, refs = refs[:partial], refs[partial:]
    outs, (xd, *acts) = refs[:6], refs[6:]
    part = pieces[0].shape[0]
    width, ff = outs[0].shape
    step = 256
    for index, piece in enumerate(pieces):
        xd[index * part:(index + 1) * part, :] = piece[...]
    for at, here, value in groups_of(firsts, z_ref, segments):
        for index in range(3):
            acts[index][here, pl.ds(at, ff // 4)] = value(index)

    def features(side):
        def body(n, carry):
            at = pl.multiple_of(n * step, step)
            x = xd[:, pl.ds(side * width + at, step)]
            dy = xd[:, pl.ds((2 + side) * width + at, step)]
            here, there = (pl.ds(at, step), slice(None)), (slice(None), pl.ds(at, step))
            values = dot(x, acts[2][...], 0, 0), dot(x, acts[1][...], 0, 0), dot(acts[0][...], dy, 0, 0)
            for index, (place, value) in enumerate(zip((here, here, there), values)):
                if partial:
                    value = value + before[3 * side + index][place].astype(F32)
                outs[3 * side + index][place] = value.astype(BF)
            return carry

        lax.fori_loop(0, width // step, body, 0)

    features(0)
    features(1)


def weight_grad(z, pieces, segments, before=()):
    firsts, arrays = firsts_and_arrays(segments)
    ff = 4 * (arrays[0].shape[1] // 3)
    part, lanes = pieces[0].shape
    rows, width = part * len(pieces), lanes // 4
    outs = [jax.ShapeDtypeStruct(shape, BF) for shape in ((width, ff), (width, ff), (ff, width))] * 2
    return pl.pallas_call(
        lambda *refs: weight_grad_kernel(firsts, len(pieces), len(before), *refs),
        in_specs=[IN_SMEM] + [IN_VMEM] * (len(pieces) + len(arrays) + len(before)),
        out_specs=[IN_VMEM] * len(outs),
        scratch_shapes=[pltpu.VMEM((rows, lanes), BF)] + [pltpu.VMEM((rows, ff), BF)] * 3,
        out_shape=outs,
        compiler_params=pltpu.CompilerParams(vmem_limit_bytes=12 * 2**20),
        cost_estimate=cost(12 * rows * width * ff, 2 * (rows * lanes + 6 * width * ff)),
    )(z, *pieces, *arrays, *before)


def weight_sum_kernel(*refs):
    for own, other, out in zip(refs[:3], refs[3:6], refs[6:]):
        out[...] = (own[...].astype(F32) + other[...].astype(F32)).astype(BF)


def weight_sum(own, other):
    steps = 4
    specs = [pl.BlockSpec((value.shape[0] // steps, value.shape[1]), lambda n: (n, 0)) for value in own]
    return pl.pallas_call(
        weight_sum_kernel,
        grid=(steps,),
        in_specs=specs * 2,
        out_specs=specs,
        out_shape=[jax.ShapeDtypeStruct(value.shape, BF) for value in own],
        compiler_params=pltpu.CompilerParams(vmem_limit_bytes=8 * 2**20),
        cost_estimate=cost(3 * own[0].size, 18 * own[0].size),
    )(*own, *other)


def from_x(value, k):
    return lax.ppermute(value, "rows", [((i + k) % 4, i) for i in range(4)])


def from_y(value, k):
    return lax.ppermute(value, "hid", [((i + 2 * k) % 8, i) for i in range(8)])


def swap_x(value, k):
    return lax.ppermute(value, "rows", [(i ^ k, i) for i in range(4)])


def swap_y(value, k):
    return lax.ppermute(value, "hid", [(i ^ (2 * k), i) for i in range(8)])


def swap_z(value, k):
    return lax.ppermute(value, "wid", [(i ^ (2 * k), i) for i in range(8)])


def from_core(value):
    return lax.ppermute(value, "wid", [(i ^ 1, i) for i in range(8)])


def from_zlo(value):
    return lax.ppermute(value, "hid", [(i ^ 1, i) for i in range(8)])


def from_corner(value):
    return lax.ppermute(value, ("hid", "wid"), [(i ^ 9, i) for i in range(64)])


def add(*values):
    total = values[0].astype(F32)
    for value in values[1:]:
        total = total + value.astype(F32)
    return total.astype(BF)


def after(value, *others):
    return lax.optimization_barrier((value, others))[0]


def first_step(first, z, pieces, weights):
    keep, later, send = forward(first, z, pieces, weights)
    return keep, later, swap_z(send, first)


def second_step(first, product):
    keep, later, got = product
    return keep, got, swap_z(add(later, got[keep.shape[0]:]), 4 - first)


def paired(mine, got):
    return jnp.concatenate([mine, got], axis=0)


def held(segments, others):
    firsts, arrays = firsts_and_arrays(segments)
    arrays = after(arrays, others)
    return [(first, *arrays[2 * i:2 * i + 2]) for i, first in enumerate(firsts)]


def double(value, swap):
    pair = jnp.concatenate([value, swap(value, 1)], axis=0)
    return jnp.concatenate([pair, swap(pair, 3)], axis=0)


def local(tokens, grad_out, gate_weight, up_weight, down_weight):
    wid = lax.axis_index("wid")
    core = lax.rem(wid, 2)
    z = (wid // 2).astype(jnp.int32).reshape(1)
    n = tokens.shape[0] // 2
    width = tokens.shape[1]

    both = jnp.concatenate([tokens, grad_out], axis=1)
    mine = lax.dynamic_slice_in_dim(both, core * n, n, 0)
    rest = lax.dynamic_slice_in_dim(both, (1 - core) * n, n, 0)
    r_core, r_zlo, r_corner = from_core(rest), from_zlo(mine), from_corner(rest)
    swapped = [from_core(weight) for weight in (gate_weight, up_weight, down_weight)]

    def lay(own, other):
        return jnp.concatenate([own[:, :width], other[:, :width], own[:, width:], other[:, width:]], axis=1)

    a, b = lay(mine, r_core), lay(r_zlo, r_corner)
    b, wg2, wu2, wd2 = lax.optimization_barrier((b, *swapped))
    weights = (gate_weight, wg2, up_weight, wu2, down_weight, wd2)

    a, b = lax.optimization_barrier((double(a, swap_x), double(b, swap_y)))
    plus = [from_y(a, 1), from_x(b, 1)]
    minus = [from_y(a, -1), from_x(b, -1)]

    pairing = (1, 3)
    own_p = [first_step(first, z, [piece], weights) for first, piece in zip(pairing, (a, b))]
    plus = after(plus, own_p[0][2], own_p[1][2])
    far = [from_y(plus[0], 1), from_x(plus[1], 1)]
    minus = after(minus, plus)
    own_q = [second_step(first, product) for first, product in zip(pairing, own_p)]
    side_p = [first_step(1, z, minus, weights)]
    side_p.append(first_step(3, z, after(plus, own_q[0][2], own_q[1][2], side_p[0][0]), weights))
    own_h = [swiglu(*after(product, side_p[0][0])) for product in own_q]
    own_pair = [paired(mine, swap_z(mine, first)) for first, mine in zip(pairing, own_h)]

    side_p = after(side_p, own_pair)
    side_q = [second_step(first, product) for first, product in zip(pairing, side_p)]
    far_p = [first_step(first, z, [after(piece, side_p[0][2], side_p[1][2])], weights) for first, piece in zip(pairing, far)]
    side_h = [swiglu(*after(product, far_p[0][0], far_p[1][0])) for product in side_q]
    far_p = after(far_p, side_h)
    far_q = [second_step(first, product) for first, product in zip(pairing, far_p)]
    side_got = [swap_z(mine, first) for first, mine in zip(pairing, side_h)]
    side_pair = [paired(mine, after(got, far_p[0][2], far_p[1][2])) for mine, got in zip(side_h, side_got)]
    far_h = [swiglu(*after(product, side_pair)) for product in far_q]
    own_s = [(first, pair, swap_z(pair, 4 - first)) for first, pair in zip(pairing, own_pair)]
    side_s = [(first, pair, swap_z(pair, 4 - first)) for first, pair in zip(pairing, side_pair)]
    own_a, own_b = input_grad(z, held(own_s, far_h), weights)
    far_got = [swap_z(mine, first) for first, mine in zip(pairing, far_h)]
    far_pair = [paired(mine, after(got, own_a)) for mine, got in zip(far_h, far_got)]
    first_grads = weight_grad(z, [a, b], held(own_s, far_pair))
    side_s = held(side_s, first_grads)
    far_pair = after(far_pair, side_s[0][2], side_s[1][2])
    far_s = [(first, pair, swap_z(pair, 4 - first)) for first, pair in zip(pairing, far_pair)]

    minus_a, minus_b = input_grad(z, side_s[:1], weights)
    plus_a, plus_b = input_grad(z, side_s[1:], weights)
    far_a, far_b = input_grad(z, held(far_s, (minus_a, plus_a)), weights)
    plus_a, plus_b = add(plus_a, from_y(far_a, -1)), add(plus_b, from_x(far_b, -1))
    minus_a, minus_b = from_y(minus_a, 1), from_x(minus_b, 1)

    segments = held(side_s + far_s, (plus_a, plus_b, minus_a, minus_b))
    keep_and_send = weight_grad(z, [*minus, *plus, *far], segments, first_grads)
    late = [from_core(value) for value in keep_and_send[3:]]
    grads = weight_sum(keep_and_send[:3], late)

    sa = add(own_a, minus_a, from_y(plus_a, -1))
    sb = add(own_b, minus_b, from_x(plus_b, -1))
    half = sa.shape[0] // 2
    got_a, got_b = swap_x(sa[half:], 3), swap_y(sb[half:], 3)
    pa, pb = add(sa[:half], got_a), add(sb[:half], got_b)
    fa = add(pa[:n], after(swap_x(pa[n:], 1), late))
    fb = add(pb[:n], after(swap_y(pb[n:], 1), late))
    near = add(fa[:, :width], from_zlo(fb[:, :width]))
    other = add(from_core(fa[:, width:]), from_corner(fb[:, width:]))
    first = core == 0
    grad_tokens = jnp.concatenate([jnp.where(first, near, other), jnp.where(first, other, near)], axis=0)
    return (grad_tokens, *grads)


def solution(mesh):
    return jax.shard_map(
        local,
        mesh=mesh,
        in_specs=(
            P(("rows", "hid"), "wid"),
            P(("rows", "hid"), "wid"),
            P("wid", ("rows", "hid")),
            P("wid", ("rows", "hid")),
            P(("rows", "hid"), "wid"),
        ),
        out_specs=(
            P(("rows", "hid"), "wid"),
            P("wid", ("rows", "hid")),
            P("wid", ("rows", "hid")),
            P(("rows", "hid"), "wid"),
        ),
        check_vma=False,
    )
```

```python
import jax
import jax.numpy as jnp
from jax import lax
from jax.experimental import pallas as pl
from jax.experimental.pallas import tpu as pltpu
from jax.sharding import PartitionSpec as P

BF = jnp.bfloat16
F32 = jnp.float32
IN_VMEM = pl.BlockSpec(memory_space=pltpu.VMEM)
IN_SMEM = pl.BlockSpec(memory_space=pltpu.SMEM)


def swiglu_grads(gate, up, hidden_grad):
    logistic = jax.nn.sigmoid(gate)
    activated = gate * logistic
    hidden = (activated * up).astype(BF)
    up_grad = (hidden_grad * activated).astype(BF)
    gate_grad = (hidden_grad * up * logistic * (1.0 + gate * (1.0 - logistic))).astype(BF)
    return hidden, up_grad, gate_grad


SHARE = 8


def cost(flops, moved, transcendentals=0):
    return pl.CostEstimate(flops=flops // SHARE, bytes_accessed=moved // SHARE, transcendentals=transcendentals)


def dot(left, right, cl, cr):
    return lax.dot_general(left, right, (((cl,), (cr,)), ((), ())), preferred_element_type=F32)


def forward_kernel(first, z_ref, *refs):
    *pieces, wg, wg2, wu, wu2, wd, wd2, keep, later, send, xd, res = refs
    part = pieces[0].shape[0]
    rows = part * len(pieces)
    width, ff = wg.shape
    block = ff // 4
    step = 256
    for index, piece in enumerate(pieces):
        xd[index * part:(index + 1) * part, :] = piece[...]

    def units(n, carry):
        at = pl.ds(pl.multiple_of(n * step, step), step)
        res[0, :, at] = dot(xd[:, :width], wg[:, at], 1, 0) + dot(xd[:, width:2 * width], wg2[:, at], 1, 0)
        res[1, :, at] = dot(xd[:, :width], wu[:, at], 1, 0) + dot(xd[:, width:2 * width], wu2[:, at], 1, 0)
        res[2, :, at] = dot(xd[:, 2 * width:3 * width], wd[at, :], 1, 1) + dot(xd[:, 3 * width:], wd2[at, :], 1, 1)
        return carry

    lax.fori_loop(0, ff // step, units, 0)
    for k, out, row in ((0, keep, 0), (4 - first, later, 0), (first, send, 0), (2, send, rows)):
        at = pl.ds(pl.multiple_of((z_ref[0] ^ k) * block, block), block)
        for index in range(3):
            out[row:row + rows, index * block:(index + 1) * block] = res[index, :, at].astype(out.dtype)


def forward(first, z, pieces, weights):
    part, lanes = pieces[0].shape
    width, ff = weights[0].shape
    rows, cols = part * len(pieces), 3 * ff // 4
    return pl.pallas_call(
        lambda *refs: forward_kernel(first, *refs),
        in_specs=[IN_SMEM] + [IN_VMEM] * (len(pieces) + 6),
        out_specs=[IN_VMEM] * 3,
        scratch_shapes=[pltpu.VMEM((rows, lanes), BF), pltpu.VMEM((3, rows, ff), F32)],
        out_shape=[jax.ShapeDtypeStruct((rows, cols), F32)] * 2 + [jax.ShapeDtypeStruct((2 * rows, cols), BF)],
        compiler_params=pltpu.CompilerParams(vmem_limit_bytes=8 * 2**20),
        cost_estimate=cost(12 * rows * width * ff, 2 * (6 * ff * width + rows * lanes)),
    )(z, *pieces, *weights)


def swiglu_kernel(keep, got, last, out):
    rows, cols = last.shape
    block = cols // 3
    total = keep[...] + got[:rows, :].astype(F32) + last[...].astype(F32)
    parts = swiglu_grads(total[:, :block], total[:, block:2 * block], total[:, 2 * block:])
    for index, part in enumerate(parts):
        out[:, index * block:(index + 1) * block] = part


def swiglu(keep, got, last):
    rows, cols = last.shape
    return pl.pallas_call(
        swiglu_kernel,
        out_shape=jax.ShapeDtypeStruct((rows, cols), BF),
        compiler_params=pltpu.CompilerParams(vmem_limit_bytes=8 * 2**20),
        cost_estimate=cost(20 * rows * cols, 12 * rows * cols, rows * cols),
    )(keep, got, last)


def groups_of(firsts, z_ref, refs):
    top = 0
    for first, pair, rest in zip(firsts, refs[::2], refs[1::2]):
        rows = pair.shape[0] // 2
        block = pair.shape[1] // 3
        for k, ref, row in ((0, pair, 0), (first, pair, rows), (4 - first, rest, 0), (2, rest, rows)):
            at = pl.multiple_of((z_ref[0] ^ k) * block, block)
            yield at, slice(top, top + rows), lambda index, ref=ref, row=row, rows=rows, block=block: ref[
                row:row + rows, index * block:(index + 1) * block
            ]
        top += rows


def input_grad_kernel(firsts, z_ref, *refs):
    count = 2 * len(firsts)
    segments, (wg, wg2, wu, wu2, *outs, acts) = refs[:count], refs[count:]
    part = outs[0].shape[0]
    block = segments[0].shape[1] // 3
    width, ff = wg.shape
    step = 256
    for at, here, value in groups_of(firsts, z_ref, segments):
        acts[here, pl.ds(ff + at, block)] = value(1)
        acts[here, pl.ds(at, block)] = value(2)

    for index, (gate, up) in enumerate(((wg, wu), (wg2, wu2))):
        def columns(n, carry):
            at = pl.multiple_of(n * step, step)
            res = dot(acts[:, :ff], gate[pl.ds(at, step), :], 1, 1)
            res = (res + dot(acts[:, ff:], up[pl.ds(at, step), :], 1, 1)).astype(BF)
            for place, out in enumerate(outs):
                out[:, pl.ds(index * width + at, step)] = res[place * part:(place + 1) * part]
            return carry

        lax.fori_loop(0, width // step, columns, 0)


def firsts_and_arrays(segments):
    return [first for first, *_ in segments], [array for _, *arrays in segments for array in arrays]


def input_grad(z, part, segments, weights):
    firsts, arrays = firsts_and_arrays(segments)
    rows = sum(array.shape[0] for array in arrays) // 4
    width, ff = weights[0].shape
    return pl.pallas_call(
        lambda *refs: input_grad_kernel(firsts, *refs),
        in_specs=[IN_SMEM] + [IN_VMEM] * (len(arrays) + 4),
        out_specs=[IN_VMEM] * (rows // part),
        scratch_shapes=[pltpu.VMEM((rows, 2 * ff), BF)],
        out_shape=[jax.ShapeDtypeStruct((part, 2 * width), BF)] * (rows // part),
        compiler_params=pltpu.CompilerParams(vmem_limit_bytes=8 * 2**20),
        cost_estimate=cost(8 * rows * width * ff, 4 * (2 * ff * width + rows * width)),
    )(z, *arrays, *weights[:4])


def weight_grad_kernel(firsts, count, partial, z_ref, *refs):
    pieces, refs = refs[:count], refs[count:]
    segments, refs = refs[:2 * len(firsts)], refs[2 * len(firsts):]
    before, refs = refs[:partial], refs[partial:]
    outs, (xd, *acts) = refs[:6], refs[6:]
    part = pieces[0].shape[0]
    width, ff = outs[0].shape
    step = 256
    for index, piece in enumerate(pieces):
        xd[index * part:(index + 1) * part, :] = piece[...]
    for at, here, value in groups_of(firsts, z_ref, segments):
        for index in range(3):
            acts[index][here, pl.ds(at, ff // 4)] = value(index)

    def features(side):
        def body(n, carry):
            at = pl.multiple_of(n * step, step)
            x = xd[:, pl.ds(side * width + at, step)]
            dy = xd[:, pl.ds((2 + side) * width + at, step)]
            here, there = (pl.ds(at, step), slice(None)), (slice(None), pl.ds(at, step))
            values = dot(x, acts[2][...], 0, 0), dot(x, acts[1][...], 0, 0), dot(acts[0][...], dy, 0, 0)
            for index, (place, value) in enumerate(zip((here, here, there), values)):
                if partial:
                    value = value + before[3 * side + index][place].astype(F32)
                outs[3 * side + index][place] = value.astype(BF)
            return carry

        lax.fori_loop(0, width // step, body, 0)

    features(0)
    features(1)


def weight_grad(z, pieces, segments, before=()):
    firsts, arrays = firsts_and_arrays(segments)
    ff = 4 * (arrays[0].shape[1] // 3)
    part, lanes = pieces[0].shape
    rows, width = part * len(pieces), lanes // 4
    outs = [jax.ShapeDtypeStruct(shape, BF) for shape in ((width, ff), (width, ff), (ff, width))] * 2
    return pl.pallas_call(
        lambda *refs: weight_grad_kernel(firsts, len(pieces), len(before), *refs),
        in_specs=[IN_SMEM] + [IN_VMEM] * (len(pieces) + len(arrays) + len(before)),
        out_specs=[IN_VMEM] * len(outs),
        scratch_shapes=[pltpu.VMEM((rows, lanes), BF)] + [pltpu.VMEM((rows, ff), BF)] * 3,
        out_shape=outs,
        compiler_params=pltpu.CompilerParams(vmem_limit_bytes=12 * 2**20),
        cost_estimate=cost(12 * rows * width * ff, 2 * (rows * lanes + 6 * width * ff)),
    )(z, *pieces, *arrays, *before)


def from_x(value, k):
    return lax.ppermute(value, "rows", [((i + k) % 4, i) for i in range(4)])


def from_y(value, k):
    return lax.ppermute(value, "hid", [((i + 2 * k) % 8, i) for i in range(8)])


def swap_x(value, k):
    return lax.ppermute(value, "rows", [(i ^ k, i) for i in range(4)])


def swap_y(value, k):
    return lax.ppermute(value, "hid", [(i ^ (2 * k), i) for i in range(8)])


def swap_z(value, k):
    return lax.ppermute(value, "wid", [(i ^ (2 * k), i) for i in range(8)])


def from_core(value):
    return lax.ppermute(value, "wid", [(i ^ 1, i) for i in range(8)])


def from_zlo(value):
    return lax.ppermute(value, "hid", [(i ^ 1, i) for i in range(8)])


def from_corner(value):
    return lax.ppermute(value, ("hid", "wid"), [(i ^ 9, i) for i in range(64)])


def add(*values):
    total = values[0].astype(F32)
    for value in values[1:]:
        total = total + value.astype(F32)
    return total.astype(BF)


def after(value, *others):
    return lax.optimization_barrier((value, others))[0]


def first_step(first, z, pieces, weights):
    keep, later, send = forward(first, z, pieces, weights)
    return keep, later, swap_z(send, first)


def second_step(first, product):
    keep, later, got = product
    return keep, got, swap_z(add(later, got[keep.shape[0]:]), 4 - first)


def paired(mine, got):
    return jnp.concatenate([mine, got], axis=0)


def held(segments, others):
    firsts, arrays = firsts_and_arrays(segments)
    arrays = after(arrays, others)
    return [(first, *arrays[2 * i:2 * i + 2]) for i, first in enumerate(firsts)]


def double(value, swap):
    pair = jnp.concatenate([value, swap(value, 1)], axis=0)
    return jnp.concatenate([pair, swap(pair, 3)], axis=0)


def local(tokens, grad_out, gate_weight, up_weight, down_weight):
    wid = lax.axis_index("wid")
    core = lax.rem(wid, 2)
    z = (wid // 2).astype(jnp.int32).reshape(1)
    n = tokens.shape[0] // 2
    width = tokens.shape[1]

    both = jnp.concatenate([tokens, grad_out], axis=1)
    mine = lax.dynamic_slice_in_dim(both, core * n, n, 0)
    rest = lax.dynamic_slice_in_dim(both, (1 - core) * n, n, 0)
    r_core, r_zlo, r_corner = from_core(rest), from_zlo(mine), from_corner(rest)
    swapped = [from_core(weight) for weight in (gate_weight, up_weight, down_weight)]

    def lay(own, other):
        return jnp.concatenate([own[:, :width], other[:, :width], own[:, width:], other[:, width:]], axis=1)

    a, b = lay(mine, r_core), lay(r_zlo, r_corner)
    wg2, wu2, wd2 = swapped
    weights = (gate_weight, wg2, up_weight, wu2, down_weight, wd2)

    a, b = after([double(a, swap_x), double(b, swap_y)], swapped)
    plus = [from_y(a, 1), from_x(b, 1)]
    minus = [from_y(a, -1), from_x(b, -1)]
    far = [from_y(plus[0], 1), from_x(plus[1], 1)]

    pairing = (1, 3)
    minus = after(minus, plus)
    side_p = [first_step(first, z, pieces, weights) for first, pieces in zip(pairing, (minus, plus))]
    side_q = [second_step(first, product) for first, product in zip(pairing, side_p)]
    far = after(far, side_p[0][2], side_p[1][2])
    last = [[a, far[0]], [b, far[1]]]
    last_p = [first_step(first, z, pieces, weights) for first, pieces in zip(pairing, last)]
    side_h = [swiglu(*after(product, last_p[0][0], last_p[1][0])) for product in side_q]
    side_pair = [paired(mine, swap_z(mine, first)) for first, mine in zip(pairing, side_h)]
    last_p = after(last_p, side_pair)
    last_h = [swiglu(*second_step(first, product)) for first, product in zip(pairing, last_p)]

    side_s = [(first, pair, swap_z(pair, 4 - first)) for first, pair in zip(pairing, side_pair)]
    side_s = held(side_s, last_h)
    part = a.shape[0]
    minus_a, minus_b = input_grad(z, part, side_s[:1], weights)
    plus_a, plus_b = input_grad(z, part, side_s[1:], weights)
    last_got = [swap_z(mine, first) for first, mine in zip(pairing, last_h)]
    last_pair = [paired(mine, after(got, minus_a, plus_a)) for mine, got in zip(last_h, last_got)]
    first_grads = weight_grad(z, [*minus, *plus], held(side_s, last_pair))
    last_s = [(first, pair, swap_z(pair, 4 - first)) for first, pair in zip(pairing, last_pair)]
    minus_a, minus_b = from_y(minus_a, 1), from_x(minus_b, 1)
    plus_a, plus_b = from_y(plus_a, -1), from_x(plus_b, -1)
    last_s = held(last_s, (first_grads, minus_a, minus_b, plus_a, plus_b))
    own_a, far_a, own_b, far_b = input_grad(z, part, last_s, weights)

    segments = held(last_s, own_a)
    keep_and_send = weight_grad(z, last[0] + last[1], segments, first_grads)
    late = [from_core(value) for value in keep_and_send[3:]]
    grads = [add(kept, got) for kept, got in zip(keep_and_send[:3], late)]

    sa = add(own_a, minus_a, plus_a, from_y(far_a, 2))
    sb = add(own_b, minus_b, plus_b, from_x(far_b, 2))
    half = sa.shape[0] // 2
    got_a, got_b = swap_x(sa[half:], 3), swap_y(sb[half:], 3)
    pa, pb = add(sa[:half], got_a), add(sb[:half], got_b)
    fa = add(pa[:n], after(swap_x(pa[n:], 1), late))
    fb = add(pb[:n], after(swap_y(pb[n:], 1), late))
    near = add(fa[:, :width], from_zlo(fb[:, :width]))
    other = add(from_core(fa[:, width:]), from_corner(fb[:, width:]))
    first = core == 0
    grad_tokens = jnp.concatenate([jnp.where(first, near, other), jnp.where(first, other, near)], axis=0)
    return (grad_tokens, *grads)


def solution(mesh):
    return jax.shard_map(
        local,
        mesh=mesh,
        in_specs=(
            P(("rows", "hid"), "wid"),
            P(("rows", "hid"), "wid"),
            P("wid", ("rows", "hid")),
            P("wid", ("rows", "hid")),
            P(("rows", "hid"), "wid"),
        ),
        out_specs=(
            P(("rows", "hid"), "wid"),
            P("wid", ("rows", "hid")),
            P("wid", ("rows", "hid")),
            P(("rows", "hid"), "wid"),
        ),
        check_vma=False,
    )
```

```python
import jax
import jax.numpy as jnp
from jax import lax
from jax.experimental import pallas as pl
from jax.experimental.pallas import tpu as pltpu
from jax.sharding import PartitionSpec as P

BF = jnp.bfloat16
F32 = jnp.float32
IN_VMEM = pl.BlockSpec(memory_space=pltpu.VMEM)
IN_SMEM = pl.BlockSpec(memory_space=pltpu.SMEM)


def swiglu_grads(gate, up, hidden_grad):
    logistic = jax.nn.sigmoid(gate)
    activated = gate * logistic
    hidden = (activated * up).astype(BF)
    up_grad = (hidden_grad * activated).astype(BF)
    gate_grad = (hidden_grad * up * logistic * (1.0 + gate * (1.0 - logistic))).astype(BF)
    return hidden, up_grad, gate_grad


SHARE = 8


def cost(flops, moved, transcendentals=0):
    return pl.CostEstimate(flops=flops // SHARE, bytes_accessed=moved // SHARE, transcendentals=transcendentals)


def dot(left, right, cl, cr):
    return lax.dot_general(left, right, (((cl,), (cr,)), ((), ())), preferred_element_type=F32)


def forward_kernel(first, z_ref, *refs):
    *pieces, wg, wg2, wu, wu2, wd, wd2, keep, later, send, xd, res = refs
    part = pieces[0].shape[0]
    rows = part * len(pieces)
    width, ff = wg.shape
    block = ff // 4
    step = 256
    for index, piece in enumerate(pieces):
        xd[index * part:(index + 1) * part, :] = piece[...]

    def units(n, carry):
        at = pl.ds(pl.multiple_of(n * step, step), step)
        res[0, :, at] = dot(xd[:, :width], wg[:, at], 1, 0) + dot(xd[:, width:2 * width], wg2[:, at], 1, 0)
        res[1, :, at] = dot(xd[:, :width], wu[:, at], 1, 0) + dot(xd[:, width:2 * width], wu2[:, at], 1, 0)
        res[2, :, at] = dot(xd[:, 2 * width:3 * width], wd[at, :], 1, 1) + dot(xd[:, 3 * width:], wd2[at, :], 1, 1)
        return carry

    lax.fori_loop(0, ff // step, units, 0)
    for k, out, row in ((0, keep, 0), (4 - first, later, 0), (first, send, 0), (2, send, rows)):
        at = pl.ds(pl.multiple_of((z_ref[0] ^ k) * block, block), block)
        for index in range(3):
            out[row:row + rows, index * block:(index + 1) * block] = res[index, :, at].astype(out.dtype)


def forward(first, z, pieces, weights):
    part, lanes = pieces[0].shape
    width, ff = weights[0].shape
    rows, cols = part * len(pieces), 3 * ff // 4
    return pl.pallas_call(
        lambda *refs: forward_kernel(first, *refs),
        in_specs=[IN_SMEM] + [IN_VMEM] * (len(pieces) + 6),
        out_specs=[IN_VMEM] * 3,
        scratch_shapes=[pltpu.VMEM((rows, lanes), BF), pltpu.VMEM((3, rows, ff), F32)],
        out_shape=[jax.ShapeDtypeStruct((rows, cols), F32)] * 2 + [jax.ShapeDtypeStruct((2 * rows, cols), BF)],
        compiler_params=pltpu.CompilerParams(vmem_limit_bytes=8 * 2**20),
        cost_estimate=cost(12 * rows * width * ff, 2 * (6 * ff * width + rows * lanes)),
    )(z, *pieces, *weights)


def swiglu_kernel(keep, got, last, out):
    rows, cols = last.shape
    block = cols // 3
    total = keep[...] + got[:rows, :].astype(F32) + last[...].astype(F32)
    parts = swiglu_grads(total[:, :block], total[:, block:2 * block], total[:, 2 * block:])
    for index, part in enumerate(parts):
        out[:, index * block:(index + 1) * block] = part


def swiglu(keep, got, last):
    rows, cols = last.shape
    return pl.pallas_call(
        swiglu_kernel,
        out_shape=jax.ShapeDtypeStruct((rows, cols), BF),
        compiler_params=pltpu.CompilerParams(vmem_limit_bytes=8 * 2**20),
        cost_estimate=cost(20 * rows * cols, 12 * rows * cols, rows * cols),
    )(keep, got, last)


def groups_of(firsts, z_ref, refs):
    top = 0
    for first, pair, rest in zip(firsts, refs[::2], refs[1::2]):
        rows = pair.shape[0] // 2
        block = pair.shape[1] // 3
        for k, ref, row in ((0, pair, 0), (first, pair, rows), (4 - first, rest, 0), (2, rest, rows)):
            at = pl.multiple_of((z_ref[0] ^ k) * block, block)
            yield at, slice(top, top + rows), lambda index, ref=ref, row=row, rows=rows, block=block: ref[
                row:row + rows, index * block:(index + 1) * block
            ]
        top += rows


def input_grad_kernel(firsts, z_ref, *refs):
    count = 2 * len(firsts)
    segments, (wg, wg2, wu, wu2, *outs, acts) = refs[:count], refs[count:]
    part = outs[0].shape[0]
    block = segments[0].shape[1] // 3
    width, ff = wg.shape
    step = 256
    for at, here, value in groups_of(firsts, z_ref, segments):
        acts[here, pl.ds(ff + at, block)] = value(1)
        acts[here, pl.ds(at, block)] = value(2)

    for index, (gate, up) in enumerate(((wg, wu), (wg2, wu2))):
        def columns(n, carry):
            at = pl.multiple_of(n * step, step)
            res = dot(acts[:, :ff], gate[pl.ds(at, step), :], 1, 1)
            res = (res + dot(acts[:, ff:], up[pl.ds(at, step), :], 1, 1)).astype(BF)
            for place, out in enumerate(outs):
                out[:, pl.ds(index * width + at, step)] = res[place * part:(place + 1) * part]
            return carry

        lax.fori_loop(0, width // step, columns, 0)


def firsts_and_arrays(segments):
    return [first for first, *_ in segments], [array for _, *arrays in segments for array in arrays]


def input_grad(z, part, segments, weights):
    firsts, arrays = firsts_and_arrays(segments)
    rows = sum(array.shape[0] for array in arrays) // 4
    width, ff = weights[0].shape
    return pl.pallas_call(
        lambda *refs: input_grad_kernel(firsts, *refs),
        in_specs=[IN_SMEM] + [IN_VMEM] * (len(arrays) + 4),
        out_specs=[IN_VMEM] * (rows // part),
        scratch_shapes=[pltpu.VMEM((rows, 2 * ff), BF)],
        out_shape=[jax.ShapeDtypeStruct((part, 2 * width), BF)] * (rows // part),
        compiler_params=pltpu.CompilerParams(vmem_limit_bytes=8 * 2**20),
        cost_estimate=cost(8 * rows * width * ff, 4 * (2 * ff * width + rows * width)),
    )(z, *arrays, *weights[:4])


def weight_grad_kernel(firsts, count, z_ref, *refs):
    xs, dys, refs = refs[:count], refs[count:2 * count], refs[2 * count:]
    segments, refs = refs[:2 * len(firsts)], refs[2 * len(firsts):]
    own, other, (x, dy, *acts) = refs[:3], refs[3:6], refs[6:]
    part = xs[0].shape[0]
    n = pl.program_id(0)

    @pl.when(n == 0)
    def _():
        for at, here, value in groups_of(firsts, z_ref, segments):
            for index in range(3):
                acts[index][here, pl.ds(at, acts[0].shape[1] // 4)] = value(index)

    for index in range(count):
        x[index * part:(index + 1) * part, :] = xs[index][...]
        dy[index * part:(index + 1) * part, :] = dys[index][...]
    gate = dot(x[...], acts[2][...], 0, 0).astype(BF)
    up = dot(x[...], acts[1][...], 0, 0).astype(BF)
    down = dot(acts[0][...], dy[...], 0, 0).astype(BF)

    def store(outs):
        for out, value in zip(outs, (gate, up, down)):
            out[...] = value

    pl.when(n < pl.num_programs(0) // 2)(lambda: store(own))
    pl.when(n >= pl.num_programs(0) // 2)(lambda: store(other))


def weight_grad(z, pieces, segments):
    firsts, arrays = firsts_and_arrays(segments)
    ff = 4 * (arrays[0].shape[1] // 3)
    part, lanes = pieces[0].shape
    rows, width = part * len(pieces), lanes // 4
    step = 256
    steps = 2 * width // step
    last = steps // 2 - 1
    first = lambda n: jnp.minimum(n, last)
    second = lambda n: jnp.maximum(n - last - 1, 0)

    def out_specs(place):
        tall = pl.BlockSpec((step, ff), lambda n: (place(n), 0))
        return [tall, tall, pl.BlockSpec((ff, step), lambda n: (0, place(n)))]

    return pl.pallas_call(
        lambda *refs: weight_grad_kernel(firsts, len(pieces), *refs),
        grid=(steps,),
        in_specs=[IN_SMEM]
        + [pl.BlockSpec((part, step), lambda n: (0, n))] * len(pieces)
        + [pl.BlockSpec((part, step), lambda n: (0, steps + n))] * len(pieces)
        + [pl.BlockSpec(array.shape, lambda n: (0, 0)) for array in arrays],
        out_specs=out_specs(first) + out_specs(second),
        scratch_shapes=[pltpu.VMEM((rows, step), BF)] * 2 + [pltpu.VMEM((rows, ff), BF)] * 3,
        out_shape=[jax.ShapeDtypeStruct(shape, BF) for shape in ((width, ff), (width, ff), (ff, width))] * 2,
        compiler_params=pltpu.CompilerParams(vmem_limit_bytes=20 * 2**20),
        cost_estimate=cost(12 * rows * width * ff, 2 * (rows * lanes + 6 * width * ff)),
    )(z, *pieces, *pieces, *arrays)


def from_x(value, k):
    return lax.ppermute(value, "rows", [((i + k) % 4, i) for i in range(4)])


def from_y(value, k):
    return lax.ppermute(value, "hid", [((i + 2 * k) % 8, i) for i in range(8)])


def swap_x(value, k):
    return lax.ppermute(value, "rows", [(i ^ k, i) for i in range(4)])


def swap_y(value, k):
    return lax.ppermute(value, "hid", [(i ^ (2 * k), i) for i in range(8)])


def swap_z(value, k):
    return lax.ppermute(value, "wid", [(i ^ (2 * k), i) for i in range(8)])


def from_core(value):
    return lax.ppermute(value, "wid", [(i ^ 1, i) for i in range(8)])


def from_zlo(value):
    return lax.ppermute(value, "hid", [(i ^ 1, i) for i in range(8)])


def from_corner(value):
    return lax.ppermute(value, ("hid", "wid"), [(i ^ 9, i) for i in range(64)])


def add(*values):
    total = values[0].astype(F32)
    for value in values[1:]:
        total = total + value.astype(F32)
    return total.astype(BF)


def after(value, *others):
    return lax.optimization_barrier((value, others))[0]


def first_step(first, z, pieces, weights):
    keep, later, send = forward(first, z, pieces, weights)
    return keep, later, swap_z(send, first)


def second_step(first, product):
    keep, later, got = product
    return keep, got, swap_z(add(later, got[keep.shape[0]:]), 4 - first)


def paired(mine, got):
    return jnp.concatenate([mine, got], axis=0)


def held(segments, others):
    firsts, arrays = firsts_and_arrays(segments)
    arrays = after(arrays, others)
    return [(first, *arrays[2 * i:2 * i + 2]) for i, first in enumerate(firsts)]


def double(value, swap):
    pair = jnp.concatenate([value, swap(value, 1)], axis=0)
    return jnp.concatenate([pair, swap(pair, 3)], axis=0)


def local(tokens, grad_out, gate_weight, up_weight, down_weight):
    wid = lax.axis_index("wid")
    core = lax.rem(wid, 2)
    z = (wid // 2).astype(jnp.int32).reshape(1)
    n = tokens.shape[0] // 2
    width = tokens.shape[1]

    both = jnp.concatenate([tokens, grad_out], axis=1)
    mine = lax.dynamic_slice_in_dim(both, core * n, n, 0)
    rest = lax.dynamic_slice_in_dim(both, (1 - core) * n, n, 0)
    r_core, r_zlo, r_corner = from_core(rest), from_zlo(mine), from_corner(rest)
    swapped = [from_core(weight) for weight in (gate_weight, up_weight, down_weight)]

    def lay(own, other):
        return jnp.concatenate([own[:, :width], other[:, :width], own[:, width:], other[:, width:]], axis=1)

    a, b = lay(mine, r_core), lay(r_zlo, r_corner)
    wg2, wu2, wd2 = swapped
    weights = (gate_weight, wg2, up_weight, wu2, down_weight, wd2)

    a, b = after([double(a, swap_x), double(b, swap_y)], swapped)
    plus = [from_y(a, 1), from_x(b, 1)]
    minus = [from_y(a, -1), from_x(b, -1)]

    pairing = (1, 3)
    own_p = [first_step(first, z, [piece], weights) for first, piece in zip(pairing, (a, b))]
    plus = after(plus, own_p[0][2], own_p[1][0])
    far = [from_y(plus[0], 1), from_x(plus[1], 1)]
    minus = after(minus, plus)
    side_p = [first_step(first, z, pieces, weights) for first, pieces in zip(pairing, (minus, plus))]
    own_q = [second_step(first, product) for first, product in zip(pairing, after(own_p, side_p[0][0], side_p[1][0]))]
    side_sum = [add(later, got[keep.shape[0]:]) for keep, later, got in side_p]
    side_q = [(keep, got, swap_z(total, 4 - first)) for first, (keep, _, got), total in zip(pairing, side_p, side_sum)]
    own_h = [swiglu(*after(product, side_sum)) for product in own_q]
    own_pair = [paired(mine, swap_z(mine, first)) for first, mine in zip(pairing, own_h)]

    far_p = [first_step(first, z, [after(piece, side_sum)], weights) for first, piece in zip(pairing, far)]
    side_h = [swiglu(*after(product, far_p[0][0], far_p[1][0])) for product in side_q]
    far_p = after(far_p, side_h)
    far_q = [second_step(first, product) for first, product in zip(pairing, far_p)]
    side_got = [swap_z(mine, first) for first, mine in zip(pairing, side_h)]
    side_pair = [paired(mine, after(got, far_p[0][2], far_p[1][2])) for mine, got in zip(side_h, side_got)]
    far_h = [swiglu(*after(product, side_pair)) for product in far_q]
    own_s = [(first, pair, swap_z(pair, 4 - first)) for first, pair in zip(pairing, own_pair)]
    side_s = [(first, pair, swap_z(pair, 4 - first)) for first, pair in zip(pairing, side_pair)]
    part = a.shape[0]
    own_a, own_b = input_grad(z, part, held(own_s, far_h), weights)
    far_got = [swap_z(mine, first) for first, mine in zip(pairing, far_h)]
    far_pair = [paired(mine, after(got, own_a)) for mine, got in zip(far_h, far_got)]
    far_pair = after(far_pair, side_s[0][2], side_s[1][2])
    far_s = [(first, pair, swap_z(pair, 4 - first)) for first, pair in zip(pairing, far_pair)]

    minus_a, minus_b = input_grad(z, part, side_s[:1], weights)
    plus_a, plus_b = input_grad(z, part, side_s[1:], weights)
    far_a, far_b = input_grad(z, part, held(far_s, (minus_a, plus_a)), weights)
    plus_a, plus_b = add(plus_a, from_y(far_a, -1)), add(plus_b, from_x(far_b, -1))
    minus_a, minus_b = from_y(minus_a, 1), from_x(minus_b, 1)
    segments = own_s + held(side_s + far_s, (plus_a, plus_b, minus_a, minus_b))
    weight_grads = weight_grad(z, [a, b, *minus, *plus, *far], segments)
    late = [from_core(value) for value in weight_grads[3:]]
    grads = [add(kept, got) for kept, got in zip(weight_grads[:3], late)]

    sa = add(own_a, minus_a, from_y(plus_a, -1))
    sb = add(own_b, minus_b, from_x(plus_b, -1))
    half = sa.shape[0] // 2
    got_a, got_b = swap_x(sa[half:], 3), swap_y(sb[half:], 3)
    pa, pb = add(sa[:half], got_a), add(sb[:half], got_b)
    fa = add(pa[:n], after(swap_x(pa[n:], 1), late))
    fb = add(pb[:n], after(swap_y(pb[n:], 1), late))
    near = add(fa[:, :width], from_zlo(fb[:, :width]))
    other = add(from_core(fa[:, width:]), from_corner(fb[:, width:]))
    first = core == 0
    grad_tokens = jnp.concatenate([jnp.where(first, near, other), jnp.where(first, other, near)], axis=0)
    return (grad_tokens, *grads)


def solution(mesh):
    return jax.shard_map(
        local,
        mesh=mesh,
        in_specs=(
            P(("rows", "hid"), "wid"),
            P(("rows", "hid"), "wid"),
            P("wid", ("rows", "hid")),
            P("wid", ("rows", "hid")),
            P(("rows", "hid"), "wid"),
        ),
        out_specs=(
            P(("rows", "hid"), "wid"),
            P("wid", ("rows", "hid")),
            P("wid", ("rows", "hid")),
            P(("rows", "hid"), "wid"),
        ),
        check_vma=False,
    )
```

```python
import jax
import jax.numpy as jnp
from jax import lax
from jax.experimental import pallas as pl
from jax.experimental.pallas import tpu as pltpu
from jax.sharding import PartitionSpec as P

BF = jnp.bfloat16
F32 = jnp.float32
IN_VMEM = pl.BlockSpec(memory_space=pltpu.VMEM)
IN_SMEM = pl.BlockSpec(memory_space=pltpu.SMEM)


def swiglu_grads(gate, up, hidden_grad):
    logistic = jax.nn.sigmoid(gate)
    activated = gate * logistic
    hidden = (activated * up).astype(BF)
    up_grad = (hidden_grad * activated).astype(BF)
    gate_grad = (hidden_grad * up * logistic * (1.0 + gate * (1.0 - logistic))).astype(BF)
    return hidden, up_grad, gate_grad


SHARE = 8


def cost(flops, moved, transcendentals=0):
    return pl.CostEstimate(flops=flops // SHARE, bytes_accessed=moved // SHARE, transcendentals=transcendentals)


def dot(left, right, cl, cr):
    return lax.dot_general(left, right, (((cl,), (cr,)), ((), ())), preferred_element_type=F32)


def forward_kernel(first, z_ref, *refs):
    *pieces, wg, wg2, wu, wu2, wd, wd2, keep, later, send, xd, res = refs
    part = pieces[0].shape[0]
    rows = part * len(pieces)
    width, ff = wg.shape
    block = ff // 4
    step = 256
    for index, piece in enumerate(pieces):
        xd[index * part:(index + 1) * part, :] = piece[...]

    def units(n, carry):
        at = pl.ds(pl.multiple_of(n * step, step), step)
        res[0, :, at] = dot(xd[:, :width], wg[:, at], 1, 0) + dot(xd[:, width:2 * width], wg2[:, at], 1, 0)
        res[1, :, at] = dot(xd[:, :width], wu[:, at], 1, 0) + dot(xd[:, width:2 * width], wu2[:, at], 1, 0)
        res[2, :, at] = dot(xd[:, 2 * width:3 * width], wd[at, :], 1, 1) + dot(xd[:, 3 * width:], wd2[at, :], 1, 1)
        return carry

    lax.fori_loop(0, ff // step, units, 0)
    for k, out, row in ((0, keep, 0), (4 - first, later, 0), (first, send, 0), (2, send, rows)):
        at = pl.ds(pl.multiple_of((z_ref[0] ^ k) * block, block), block)
        for index in range(3):
            out[row:row + rows, index * block:(index + 1) * block] = res[index, :, at].astype(out.dtype)


def forward(first, z, pieces, weights):
    part, lanes = pieces[0].shape
    width, ff = weights[0].shape
    rows, cols = part * len(pieces), 3 * ff // 4
    return pl.pallas_call(
        lambda *refs: forward_kernel(first, *refs),
        in_specs=[IN_SMEM] + [IN_VMEM] * (len(pieces) + 6),
        out_specs=[IN_VMEM] * 3,
        scratch_shapes=[pltpu.VMEM((rows, lanes), BF), pltpu.VMEM((3, rows, ff), F32)],
        out_shape=[jax.ShapeDtypeStruct((rows, cols), F32)] * 2 + [jax.ShapeDtypeStruct((2 * rows, cols), BF)],
        compiler_params=pltpu.CompilerParams(vmem_limit_bytes=8 * 2**20),
        cost_estimate=cost(12 * rows * width * ff, 2 * (6 * ff * width + rows * lanes)),
    )(z, *pieces, *weights)


def swiglu_kernel(keep, got, last, out):
    rows, cols = last.shape
    block = cols // 3
    total = keep[...] + got[:rows, :].astype(F32) + last[...].astype(F32)
    parts = swiglu_grads(total[:, :block], total[:, block:2 * block], total[:, 2 * block:])
    for index, part in enumerate(parts):
        out[:, index * block:(index + 1) * block] = part


def swiglu(keep, got, last):
    rows, cols = last.shape
    return pl.pallas_call(
        swiglu_kernel,
        out_shape=jax.ShapeDtypeStruct((rows, cols), BF),
        compiler_params=pltpu.CompilerParams(vmem_limit_bytes=8 * 2**20),
        cost_estimate=cost(20 * rows * cols, 12 * rows * cols, rows * cols),
    )(keep, got, last)


def groups_of(firsts, z_ref, refs):
    top = 0
    for first, pair, rest in zip(firsts, refs[::2], refs[1::2]):
        rows = pair.shape[0] // 2
        block = pair.shape[1] // 3
        for k, ref, row in ((0, pair, 0), (first, pair, rows), (4 - first, rest, 0), (2, rest, rows)):
            at = pl.multiple_of((z_ref[0] ^ k) * block, block)
            yield at, slice(top, top + rows), lambda index, ref=ref, row=row, rows=rows, block=block: ref[
                row:row + rows, index * block:(index + 1) * block
            ]
        top += rows


def input_grad_kernel(firsts, z_ref, *refs):
    count = 2 * len(firsts)
    segments, (wg, wg2, wu, wu2, *outs, acts) = refs[:count], refs[count:]
    part = outs[0].shape[0]
    block = segments[0].shape[1] // 3
    width, ff = wg.shape
    step = 256
    for at, here, value in groups_of(firsts, z_ref, segments):
        acts[here, pl.ds(ff + at, block)] = value(1)
        acts[here, pl.ds(at, block)] = value(2)

    for index, (gate, up) in enumerate(((wg, wu), (wg2, wu2))):
        def columns(n, carry):
            at = pl.multiple_of(n * step, step)
            res = dot(acts[:, :ff], gate[pl.ds(at, step), :], 1, 1)
            res = (res + dot(acts[:, ff:], up[pl.ds(at, step), :], 1, 1)).astype(BF)
            for place, out in enumerate(outs):
                out[:, pl.ds(index * width + at, step)] = res[place * part:(place + 1) * part]
            return carry

        lax.fori_loop(0, width // step, columns, 0)


def firsts_and_arrays(segments):
    return [first for first, *_ in segments], [array for _, *arrays in segments for array in arrays]


def input_grad(z, part, segments, weights):
    firsts, arrays = firsts_and_arrays(segments)
    rows = sum(array.shape[0] for array in arrays) // 4
    width, ff = weights[0].shape
    return pl.pallas_call(
        lambda *refs: input_grad_kernel(firsts, *refs),
        in_specs=[IN_SMEM] + [IN_VMEM] * (len(arrays) + 4),
        out_specs=[IN_VMEM] * (rows // part),
        scratch_shapes=[pltpu.VMEM((rows, 2 * ff), BF)],
        out_shape=[jax.ShapeDtypeStruct((part, 2 * width), BF)] * (rows // part),
        compiler_params=pltpu.CompilerParams(vmem_limit_bytes=8 * 2**20),
        cost_estimate=cost(8 * rows * width * ff, 4 * (2 * ff * width + rows * width)),
    )(z, *arrays, *weights[:4])


def weight_grad_kernel(firsts, count, z_ref, *refs):
    xs, dys, refs = refs[:count], refs[count:2 * count], refs[2 * count:]
    segments, refs = refs[:2 * len(firsts)], refs[2 * len(firsts):]
    own, other, (x, dy, *acts) = refs[:3], refs[3:6], refs[6:]
    part = xs[0].shape[0]
    n = pl.program_id(0)

    @pl.when(n == 0)
    def _():
        for at, here, value in groups_of(firsts, z_ref, segments):
            for index in range(3):
                acts[index][here, pl.ds(at, acts[0].shape[1] // 4)] = value(index)

    for index in range(count):
        x[index * part:(index + 1) * part, :] = xs[index][...]
        dy[index * part:(index + 1) * part, :] = dys[index][...]
    gate = dot(x[...], acts[2][...], 0, 0).astype(BF)
    up = dot(x[...], acts[1][...], 0, 0).astype(BF)
    down = dot(acts[0][...], dy[...], 0, 0).astype(BF)

    def store(outs):
        for out, value in zip(outs, (gate, up, down)):
            out[...] = value

    pl.when(n < pl.num_programs(0) // 2)(lambda: store(own))
    pl.when(n >= pl.num_programs(0) // 2)(lambda: store(other))


def weight_grad(z, pieces, segments):
    firsts, arrays = firsts_and_arrays(segments)
    ff = 4 * (arrays[0].shape[1] // 3)
    part, lanes = pieces[0].shape
    rows, width = part * len(pieces), lanes // 4
    step = 256
    steps = 2 * width // step
    last = steps // 2 - 1
    first = lambda n: jnp.minimum(n, last)
    second = lambda n: jnp.maximum(n - last - 1, 0)

    def out_specs(place):
        tall = pl.BlockSpec((step, ff), lambda n: (place(n), 0))
        return [tall, tall, pl.BlockSpec((ff, step), lambda n: (0, place(n)))]

    return pl.pallas_call(
        lambda *refs: weight_grad_kernel(firsts, len(pieces), *refs),
        grid=(steps,),
        in_specs=[IN_SMEM]
        + [pl.BlockSpec((part, step), lambda n: (0, n))] * len(pieces)
        + [pl.BlockSpec((part, step), lambda n: (0, steps + n))] * len(pieces)
        + [pl.BlockSpec(array.shape, lambda n: (0, 0), pipeline_mode=pl.Buffered(1)) for array in arrays],
        out_specs=out_specs(first) + out_specs(second),
        scratch_shapes=[pltpu.VMEM((rows, step), BF)] * 2 + [pltpu.VMEM((rows, ff), BF)] * 3,
        out_shape=[jax.ShapeDtypeStruct(shape, BF) for shape in ((width, ff), (width, ff), (ff, width))] * 2,
        compiler_params=pltpu.CompilerParams(vmem_limit_bytes=14 * 2**20),
        cost_estimate=cost(12 * rows * width * ff, 2 * (rows * lanes + 6 * width * ff)),
    )(z, *pieces, *pieces, *arrays)


def from_x(value, k):
    return lax.ppermute(value, "rows", [((i + k) % 4, i) for i in range(4)])


def from_y(value, k):
    return lax.ppermute(value, "hid", [((i + 2 * k) % 8, i) for i in range(8)])


def swap_x(value, k):
    return lax.ppermute(value, "rows", [(i ^ k, i) for i in range(4)])


def swap_y(value, k):
    return lax.ppermute(value, "hid", [(i ^ (2 * k), i) for i in range(8)])


def swap_z(value, k):
    return lax.ppermute(value, "wid", [(i ^ (2 * k), i) for i in range(8)])


def from_core(value):
    return lax.ppermute(value, "wid", [(i ^ 1, i) for i in range(8)])


def from_zlo(value):
    return lax.ppermute(value, "hid", [(i ^ 1, i) for i in range(8)])


def from_corner(value):
    return lax.ppermute(value, ("hid", "wid"), [(i ^ 9, i) for i in range(64)])


def add(*values):
    total = values[0].astype(F32)
    for value in values[1:]:
        total = total + value.astype(F32)
    return total.astype(BF)


def after(value, *others):
    return lax.optimization_barrier((value, others))[0]


def first_step(first, z, pieces, weights):
    keep, later, send = forward(first, z, pieces, weights)
    return keep, later, swap_z(send, first)


def second_step(first, product):
    keep, later, got = product
    return keep, got, swap_z(add(later, got[keep.shape[0]:]), 4 - first)


def paired(mine, got):
    return jnp.concatenate([mine, got], axis=0)


def held(segments, *others):
    (first, pair, rest), *more = segments
    return [(first, after(pair, *others), rest), *more]


def double(value, swap):
    pair = jnp.concatenate([value, swap(value, 1)], axis=0)
    return jnp.concatenate([pair, swap(pair, 3)], axis=0)


def local(tokens, grad_out, gate_weight, up_weight, down_weight):
    wid = lax.axis_index("wid")
    core = lax.rem(wid, 2)
    z = (wid // 2).astype(jnp.int32).reshape(1)
    n = tokens.shape[0] // 2
    width = tokens.shape[1]

    both = jnp.concatenate([tokens, grad_out], axis=1)
    mine = lax.dynamic_slice_in_dim(both, core * n, n, 0)
    rest = lax.dynamic_slice_in_dim(both, (1 - core) * n, n, 0)
    r_core, r_zlo, r_corner = from_core(rest), from_zlo(mine), from_corner(rest)
    swapped = [from_core(weight) for weight in (gate_weight, up_weight, down_weight)]

    def lay(own, other):
        return jnp.concatenate([own[:, :width], other[:, :width], own[:, width:], other[:, width:]], axis=1)

    a, b = lay(mine, r_core), lay(r_zlo, r_corner)
    wg2, wu2, wd2 = swapped
    weights = (gate_weight, wg2, up_weight, wu2, down_weight, wd2)

    a, b = after([double(a, swap_x), double(b, swap_y)], swapped)
    plus = [from_y(a, 1), from_x(b, 1)]
    minus = [from_y(a, -1), from_x(b, -1)]

    pairing = (1, 3)
    own_p = [first_step(first, z, [piece], weights) for first, piece in zip(pairing, (a, b))]
    plus = after(plus, own_p[0][2], own_p[1][0])
    far = [from_y(plus[0], 1), from_x(plus[1], 1)]
    minus = [after(minus[0], plus), minus[1]]
    side_p = [first_step(first, z, pieces, weights) for first, pieces in zip(pairing, (minus, plus))]
    own_q = [second_step(first, product) for first, product in zip(pairing, after(own_p, side_p[0][0], side_p[1][0]))]
    side_sum = [add(later, got[keep.shape[0]:]) for keep, later, got in side_p]
    side_q = [(keep, got, swap_z(total, 4 - first)) for first, (keep, _, got), total in zip(pairing, side_p, side_sum)]
    own_h = [swiglu(*after(product, side_sum)) for product in own_q]
    own_pair = [paired(mine, swap_z(mine, first)) for first, mine in zip(pairing, own_h)]

    far_p = [first_step(first, z, [after(piece, side_sum)], weights) for first, piece in zip(pairing, far)]
    side_h = [swiglu(*after(product, far_p[0][0], far_p[1][0])) for product in side_q]
    far_p = after(far_p, side_h)
    far_q = [second_step(first, product) for first, product in zip(pairing, far_p)]
    side_got = [swap_z(mine, first) for first, mine in zip(pairing, side_h)]
    side_pair = [paired(mine, after(got, far_p[0][2], far_p[1][2])) for mine, got in zip(side_h, side_got)]
    far_h = [swiglu(*after(product, side_pair)) for product in far_q]
    own_s = [(first, pair, swap_z(pair, 4 - first)) for first, pair in zip(pairing, own_pair)]
    side_s = [(first, pair, swap_z(pair, 4 - first)) for first, pair in zip(pairing, side_pair)]
    part = a.shape[0]
    own_a, own_b = input_grad(z, part, held(own_s, far_h), weights)
    far_got = [swap_z(mine, first) for first, mine in zip(pairing, far_h)]
    far_pair = [paired(mine, after(got, own_a)) for mine, got in zip(far_h, far_got)]
    far_pair = after(far_pair, side_s[0][2], side_s[1][2])
    far_s = [(first, pair, swap_z(pair, 4 - first)) for first, pair in zip(pairing, far_pair)]

    minus_a, minus_b = input_grad(z, part, side_s[:1], weights)
    plus_a, plus_b = input_grad(z, part, side_s[1:], weights)
    far_a, far_b = input_grad(z, part, held(far_s, (minus_a, plus_a)), weights)
    plus_a, plus_b = add(plus_a, from_y(far_a, -1)), add(plus_b, from_x(far_b, -1))
    minus_a, minus_b = from_y(minus_a, 1), from_x(minus_b, 1)
    segments = held(own_s, plus_a, plus_b, minus_a, minus_b) + side_s + far_s
    weight_grads = weight_grad(z, [a, b, *minus, *plus, *far], segments)
    late = [from_core(value) for value in weight_grads[3:]]
    grads = [add(kept, got) for kept, got in zip(weight_grads[:3], late)]

    sa = add(own_a, minus_a, from_y(plus_a, -1))
    sb = add(own_b, minus_b, from_x(plus_b, -1))
    half = sa.shape[0] // 2
    got_a, got_b = swap_x(sa[half:], 3), swap_y(sb[half:], 3)
    pa, pb = add(sa[:half], got_a), add(sb[:half], got_b)
    fa = add(pa[:n], after(swap_x(pa[n:], 1), late))
    fb = add(pb[:n], after(swap_y(pb[n:], 1), late))
    near = add(fa[:, :width], from_zlo(fb[:, :width]))
    other = add(from_core(fa[:, width:]), from_corner(fb[:, width:]))
    first = core == 0
    grad_tokens = jnp.concatenate([jnp.where(first, near, other), jnp.where(first, other, near)], axis=0)
    return (grad_tokens, *grads)


def solution(mesh):
    return jax.shard_map(
        local,
        mesh=mesh,
        in_specs=(
            P(("rows", "hid"), "wid"),
            P(("rows", "hid"), "wid"),
            P("wid", ("rows", "hid")),
            P("wid", ("rows", "hid")),
            P(("rows", "hid"), "wid"),
        ),
        out_specs=(
            P(("rows", "hid"), "wid"),
            P("wid", ("rows", "hid")),
            P("wid", ("rows", "hid")),
            P(("rows", "hid"), "wid"),
        ),
        check_vma=False,
    )
```

```python
import jax
import jax.numpy as jnp
from jax import lax
from jax.experimental import pallas as pl
from jax.experimental.pallas import tpu as pltpu
from jax.sharding import PartitionSpec as P

BF = jnp.bfloat16
F32 = jnp.float32
IN_VMEM = pl.BlockSpec(memory_space=pltpu.VMEM)
IN_SMEM = pl.BlockSpec(memory_space=pltpu.SMEM)


def swiglu_grads(gate, up, hidden_grad):
    logistic = jax.nn.sigmoid(gate)
    activated = gate * logistic
    hidden = (activated * up).astype(BF)
    up_grad = (hidden_grad * activated).astype(BF)
    gate_grad = (hidden_grad * up * logistic * (1.0 + gate * (1.0 - logistic))).astype(BF)
    return hidden, up_grad, gate_grad


SHARE = 8


def cost(flops, moved, transcendentals=0):
    return pl.CostEstimate(flops=flops // SHARE, bytes_accessed=moved // SHARE, transcendentals=transcendentals)


def dot(left, right, cl, cr):
    return lax.dot_general(left, right, (((cl,), (cr,)), ((), ())), preferred_element_type=F32)


def forward_kernel(first, z_ref, *refs):
    *pieces, wg, wg2, wu, wu2, wd, wd2, keep, later, send, xd, res = refs
    part = pieces[0].shape[0]
    rows = part * len(pieces)
    width, ff = wg.shape
    block = ff // 4
    step = 256
    for index, piece in enumerate(pieces):
        xd[index * part:(index + 1) * part, :] = piece[...]

    def units(n, carry):
        at = pl.ds(pl.multiple_of(n * step, step), step)
        res[0, :, at] = dot(xd[:, :width], wg[:, at], 1, 0) + dot(xd[:, width:2 * width], wg2[:, at], 1, 0)
        res[1, :, at] = dot(xd[:, :width], wu[:, at], 1, 0) + dot(xd[:, width:2 * width], wu2[:, at], 1, 0)
        res[2, :, at] = dot(xd[:, 2 * width:3 * width], wd[at, :], 1, 1) + dot(xd[:, 3 * width:], wd2[at, :], 1, 1)
        return carry

    lax.fori_loop(0, ff // step, units, 0)
    for k, out, row in ((0, keep, 0), (4 - first, later, 0), (first, send, 0), (2, send, rows)):
        at = pl.ds(pl.multiple_of((z_ref[0] ^ k) * block, block), block)
        for index in range(3):
            out[row:row + rows, index * block:(index + 1) * block] = res[index, :, at].astype(out.dtype)


def forward(first, z, pieces, weights):
    part, lanes = pieces[0].shape
    width, ff = weights[0].shape
    rows, cols = part * len(pieces), 3 * ff // 4
    return pl.pallas_call(
        lambda *refs: forward_kernel(first, *refs),
        in_specs=[IN_SMEM] + [IN_VMEM] * (len(pieces) + 6),
        out_specs=[IN_VMEM] * 3,
        scratch_shapes=[pltpu.VMEM((rows, lanes), BF), pltpu.VMEM((3, rows, ff), F32)],
        out_shape=[jax.ShapeDtypeStruct((rows, cols), F32)] * 2 + [jax.ShapeDtypeStruct((2 * rows, cols), BF)],
        compiler_params=pltpu.CompilerParams(vmem_limit_bytes=8 * 2**20),
        cost_estimate=cost(12 * rows * width * ff, 2 * (6 * ff * width + rows * lanes)),
    )(z, *pieces, *weights)


def swiglu_kernel(keep, got, last, out):
    rows, cols = last.shape
    block = cols // 3
    total = keep[...] + got[:rows, :].astype(F32) + last[...].astype(F32)
    parts = swiglu_grads(total[:, :block], total[:, block:2 * block], total[:, 2 * block:])
    for index, part in enumerate(parts):
        out[:, index * block:(index + 1) * block] = part


def swiglu(keep, got, last):
    rows, cols = last.shape
    return pl.pallas_call(
        swiglu_kernel,
        out_shape=jax.ShapeDtypeStruct((rows, cols), BF),
        compiler_params=pltpu.CompilerParams(vmem_limit_bytes=8 * 2**20),
        cost_estimate=cost(20 * rows * cols, 12 * rows * cols, rows * cols),
    )(keep, got, last)


def groups_of(firsts, z_ref, refs):
    top = 0
    for first, pair, rest in zip(firsts, refs[::2], refs[1::2]):
        rows = pair.shape[0] // 2
        block = pair.shape[1] // 3
        for k, ref, row in ((0, pair, 0), (first, pair, rows), (4 - first, rest, 0), (2, rest, rows)):
            at = pl.multiple_of((z_ref[0] ^ k) * block, block)
            yield at, slice(top, top + rows), lambda index, ref=ref, row=row, rows=rows, block=block: ref[
                row:row + rows, index * block:(index + 1) * block
            ]
        top += rows


def input_grad_kernel(firsts, z_ref, *refs):
    count = 2 * len(firsts)
    segments, (wg, wg2, wu, wu2, *outs, acts) = refs[:count], refs[count:]
    part = outs[0].shape[0]
    block = segments[0].shape[1] // 3
    width, ff = wg.shape
    step = 256
    for at, here, value in groups_of(firsts, z_ref, segments):
        acts[here, pl.ds(ff + at, block)] = value(1)
        acts[here, pl.ds(at, block)] = value(2)

    for index, (gate, up) in enumerate(((wg, wu), (wg2, wu2))):
        def columns(n, carry):
            at = pl.multiple_of(n * step, step)
            res = dot(acts[:, :ff], gate[pl.ds(at, step), :], 1, 1)
            res = (res + dot(acts[:, ff:], up[pl.ds(at, step), :], 1, 1)).astype(BF)
            for place, out in enumerate(outs):
                out[:, pl.ds(index * width + at, step)] = res[place * part:(place + 1) * part]
            return carry

        lax.fori_loop(0, width // step, columns, 0)


def firsts_and_arrays(segments):
    return [first for first, *_ in segments], [array for _, *arrays in segments for array in arrays]


def input_grad(z, part, segments, weights):
    firsts, arrays = firsts_and_arrays(segments)
    rows = sum(array.shape[0] for array in arrays) // 4
    width, ff = weights[0].shape
    return pl.pallas_call(
        lambda *refs: input_grad_kernel(firsts, *refs),
        in_specs=[IN_SMEM] + [IN_VMEM] * (len(arrays) + 4),
        scratch_shapes=[pltpu.VMEM((rows, 2 * ff), BF)],
        out_shape=[jax.ShapeDtypeStruct((part, 2 * width), BF)] * (rows // part),
        compiler_params=pltpu.CompilerParams(vmem_limit_bytes=8 * 2**20),
        cost_estimate=cost(8 * rows * width * ff, 4 * (2 * ff * width + rows * width)),
    )(z, *arrays, *weights[:4])


def weight_grad_kernel(firsts, count, z_ref, *refs):
    xs, dys, refs = refs[:count], refs[count:2 * count], refs[2 * count:]
    segments, refs = refs[:2 * len(firsts)], refs[2 * len(firsts):]
    own, other, (x, dy, *acts) = refs[:3], refs[3:6], refs[6:]
    part = xs[0].shape[0]
    n = pl.program_id(0)

    @pl.when(n == 0)
    def _():
        for at, here, value in groups_of(firsts, z_ref, segments):
            for index in range(3):
                acts[index][here, pl.ds(at, acts[0].shape[1] // 4)] = value(index)

    for index in range(count):
        x[index * part:(index + 1) * part, :] = xs[index][...]
        dy[index * part:(index + 1) * part, :] = dys[index][...]
    gate = dot(x[...], acts[2][...], 0, 0).astype(BF)
    up = dot(x[...], acts[1][...], 0, 0).astype(BF)
    down = dot(acts[0][...], dy[...], 0, 0).astype(BF)

    def store(outs):
        for out, value in zip(outs, (gate, up, down)):
            out[...] = value

    pl.when(n < pl.num_programs(0) // 2)(lambda: store(own))
    pl.when(n >= pl.num_programs(0) // 2)(lambda: store(other))


def weight_grad(z, pieces, segments):
    firsts, arrays = firsts_and_arrays(segments)
    ff = 4 * (arrays[0].shape[1] // 3)
    part, lanes = pieces[0].shape
    rows, width = part * len(pieces), lanes // 4
    step = 256
    steps = 2 * width // step
    last = steps // 2 - 1
    first = lambda n: jnp.minimum(n, last)
    second = lambda n: jnp.maximum(n - last - 1, 0)

    def out_specs(place):
        tall = pl.BlockSpec((step, ff), lambda n: (place(n), 0))
        return [tall, tall, pl.BlockSpec((ff, step), lambda n: (0, place(n)))]

    return pl.pallas_call(
        lambda *refs: weight_grad_kernel(firsts, len(pieces), *refs),
        grid=(steps,),
        in_specs=[IN_SMEM]
        + [pl.BlockSpec((part, step), lambda n: (0, n))] * len(pieces)
        + [pl.BlockSpec((part, step), lambda n: (0, steps + n))] * len(pieces)
        + [pl.BlockSpec(array.shape, lambda n: (0, 0), pipeline_mode=pl.Buffered(1)) for array in arrays],
        out_specs=out_specs(first) + out_specs(second),
        scratch_shapes=[pltpu.VMEM((rows, step), BF)] * 2 + [pltpu.VMEM((rows, ff), BF)] * 3,
        out_shape=[jax.ShapeDtypeStruct(shape, BF) for shape in ((width, ff), (width, ff), (ff, width))] * 2,
        compiler_params=pltpu.CompilerParams(vmem_limit_bytes=14 * 2**20),
        cost_estimate=cost(12 * rows * width * ff, 2 * (rows * lanes + 6 * width * ff)),
    )(z, *pieces, *pieces, *arrays)


def from_x(value, k):
    return lax.ppermute(value, "rows", [((i + k) % 4, i) for i in range(4)])


def from_y(value, k):
    return lax.ppermute(value, "hid", [((i + 2 * k) % 8, i) for i in range(8)])


def swap_x(value, k):
    return lax.ppermute(value, "rows", [(i ^ k, i) for i in range(4)])


def swap_y(value, k):
    return lax.ppermute(value, "hid", [(i ^ (2 * k), i) for i in range(8)])


def swap_z(value, k):
    return lax.ppermute(value, "wid", [(i ^ (2 * k), i) for i in range(8)])


def from_core(value):
    return lax.ppermute(value, "wid", [(i ^ 1, i) for i in range(8)])


def from_zlo(value):
    return lax.ppermute(value, "hid", [(i ^ 1, i) for i in range(8)])


def from_corner(value):
    return lax.ppermute(value, ("hid", "wid"), [(i ^ 9, i) for i in range(64)])


def add(*values):
    total = values[0].astype(F32)
    for value in values[1:]:
        total = total + value.astype(F32)
    return total.astype(BF)


def after(value, *others):
    return lax.optimization_barrier((value, others))[0]


def first_step(first, z, pieces, weights):
    keep, later, send = forward(first, z, pieces, weights)
    return keep, later, swap_z(send, first)


def second_step(first, product):
    keep, later, got = product
    return keep, got, swap_z(add(later, got[keep.shape[0]:]), 4 - first)


def paired(mine, got):
    return jnp.concatenate([mine, got], axis=0)


def held(segments, *others):
    (first, pair, rest), *more = segments
    return [(first, after(pair, *others), rest), *more]


def double(value, swap):
    pair = jnp.concatenate([value, swap(value, 1)], axis=0)
    return jnp.concatenate([pair, swap(pair, 3)], axis=0)


def local(tokens, grad_out, gate_weight, up_weight, down_weight):
    wid = lax.axis_index("wid")
    core = lax.rem(wid, 2)
    z = (wid // 2).astype(jnp.int32).reshape(1)
    n = tokens.shape[0] // 2
    width = tokens.shape[1]

    both = jnp.concatenate([tokens, grad_out], axis=1)
    mine = lax.dynamic_slice_in_dim(both, core * n, n, 0)
    rest = lax.dynamic_slice_in_dim(both, (1 - core) * n, n, 0)
    r_core, r_zlo, r_corner = from_core(rest), from_zlo(mine), from_corner(rest)
    swapped = [from_core(weight) for weight in (gate_weight, up_weight, down_weight)]

    def lay(own, other):
        return jnp.concatenate([own[:, :width], other[:, :width], own[:, width:], other[:, width:]], axis=1)

    a, b = lay(mine, r_core), lay(r_zlo, r_corner)
    wg2, wu2, wd2 = swapped
    weights = (gate_weight, wg2, up_weight, wu2, down_weight, wd2)

    a, b = after([double(a, swap_x), double(b, swap_y)], swapped)
    plus = [from_y(a, 1), from_x(b, 1)]
    minus = [from_y(a, -1), from_x(b, -1)]

    pairing = (1, 3)
    own_p = [first_step(first, z, [piece], weights) for first, piece in zip(pairing, (a, b))]
    plus = after(plus, own_p[0][2], own_p[1][0])
    far = [from_y(plus[0], 1), from_x(plus[1], 1)]
    minus = [after(minus[0], plus), minus[1]]
    side_p = [first_step(first, z, pieces, weights) for first, pieces in zip(pairing, (minus, plus))]
    own_q = [second_step(first, product) for first, product in zip(pairing, after(own_p, side_p[0][0], side_p[1][0]))]
    side_sum = [add(later, got[keep.shape[0]:]) for keep, later, got in side_p]
    side_q = [(keep, got, swap_z(total, 4 - first)) for first, (keep, _, got), total in zip(pairing, side_p, side_sum)]
    own_h = [swiglu(*after(product, side_sum)) for product in own_q]
    own_pair = [paired(mine, swap_z(mine, first)) for first, mine in zip(pairing, own_h)]

    far_p = [first_step(first, z, [after(piece, side_sum)], weights) for first, piece in zip(pairing, far)]
    side_h = [swiglu(*after(product, far_p[0][0], far_p[1][0])) for product in side_q]
    far_p = after(far_p, side_h)
    far_q = [second_step(first, product) for first, product in zip(pairing, far_p)]
    side_got = [swap_z(mine, first) for first, mine in zip(pairing, side_h)]
    side_pair = [paired(mine, after(got, far_p[0][2], far_p[1][2])) for mine, got in zip(side_h, side_got)]
    far_h = [swiglu(*after(product, side_pair)) for product in far_q]
    own_s = [(first, pair, swap_z(pair, 4 - first)) for first, pair in zip(pairing, own_pair)]
    side_s = [(first, pair, swap_z(pair, 4 - first)) for first, pair in zip(pairing, side_pair)]
    part = a.shape[0]
    own_a, own_b = input_grad(z, part, held(own_s, far_h), weights)
    far_got = [swap_z(mine, first) for first, mine in zip(pairing, far_h)]
    far_pair = [paired(mine, after(got, own_a)) for mine, got in zip(far_h, far_got)]
    far_pair = after(far_pair, side_s[0][2], side_s[1][2])
    far_s = [(first, pair, swap_z(pair, 4 - first)) for first, pair in zip(pairing, far_pair)]

    minus_a, minus_b = input_grad(z, part, side_s[:1], weights)
    plus_a, plus_b = input_grad(z, part, side_s[1:], weights)
    far_a, far_b = input_grad(z, part, held(far_s, (minus_a, plus_a)), weights)
    plus_a, plus_b = add(plus_a, from_y(far_a, -1)), add(plus_b, from_x(far_b, -1))
    minus_a, minus_b = from_y(minus_a, 1), from_x(minus_b, 1)
    segments = held(own_s, plus_a, plus_b, minus_a, minus_b) + side_s + far_s
    weight_grads = weight_grad(z, [a, b, *minus, *plus, *far], segments)
    late = [from_core(value) for value in weight_grads[3:]]
    grads = [add(kept, got) for kept, got in zip(weight_grads[:3], late)]

    sa = add(own_a, minus_a, from_y(plus_a, -1))
    sb = add(own_b, minus_b, from_x(plus_b, -1))
    half = sa.shape[0] // 2
    got_a, got_b = swap_x(sa[half:], 3), swap_y(sb[half:], 3)
    pa, pb = add(sa[:half], got_a), add(sb[:half], got_b)
    fa = add(pa[:n], after(swap_x(pa[n:], 1), late))
    fb = add(pb[:n], after(swap_y(pb[n:], 1), late))
    near = add(fa[:, :width], from_zlo(fb[:, :width]))
    other = add(from_core(fa[:, width:]), from_corner(fb[:, width:]))
    first = core == 0
    grad_tokens = jnp.concatenate([jnp.where(first, near, other), jnp.where(first, other, near)], axis=0)
    return (grad_tokens, *grads)


def solution(mesh):
    return jax.shard_map(
        local,
        mesh=mesh,
        in_specs=(
            P(("rows", "hid"), "wid"),
            P(("rows", "hid"), "wid"),
            P("wid", ("rows", "hid")),
            P("wid", ("rows", "hid")),
            P(("rows", "hid"), "wid"),
        ),
        out_specs=(
            P(("rows", "hid"), "wid"),
            P("wid", ("rows", "hid")),
            P("wid", ("rows", "hid")),
            P(("rows", "hid"), "wid"),
        ),
        check_vma=False,
    )
```
